32 devices in a mesh: cuts: 4 (over y, x), azim: 8 (over z, core).
Axes of the slice: x: 2, y: 2, z: 4, core: 2. Of those that a mesh axis runs over, the one named last changes fastest.
Arguments:
- potential: float32 [8, 1024, 4096], P('cuts', None, 'azim'), may hold values from -3 to 3
- direction: float32 [8, 1024, 4096], P('cuts', None, 'azim'), may hold values from -6 to 6
- source: float32 [8, 1024, 4096], P('cuts', None, 'azim'), may hold values from -6 to 6
- region_ids: int32 [8, 1024, 4096], P('cuts', None, 'azim'), may hold values from 0 to 7
- table_ids: int32 [8, 1024, 4096], P('cuts', None, 'azim'), may hold values from 0 to 15
- region_reluct: float32 [8], replicated, may hold values from 0.2 to 2
- table_sat: float32 [16], replicated, may hold values from 0.05 to 1
- skew_offsets: int32 [8], P('cuts'), may hold values from 0 to 4095
Outputs:
- residual: float32 [8, 1024, 4096], P('cuts', None, 'azim')
- jac_product: float32 [8, 1024, 4096], P('cuts', None, 'azim')
- gap_flux: float32 [2, 8, 2, 4096], P(None, 'cuts', None, 'azim')
The draws below stay inside these ranges and needn't reach their ends.
Inputs may be any that keep to these rules, and one draw needn't show every extreme that they name: `region_ids`: each cell names one of the 8 material regions. `table_ids`: each cell names one of the 16 saturation entries.
All inputs are finite; a program needn't handle non-finite values.
Results may differ from the reference program's by a relative error of at most 0.000082.
Values sent between devices are 32-bit elements; how exact they have to be, the bound alone decides.
A program may use at most 192 MiB of HBM per device.

```python
import math
import jax
import jax.numpy as jnp
from jax import lax

R = 1024
P_SIZE = 4096
NREG = 8
NTAB = 16
M = 2048
RG = 512
SLICES = 8


def touch_ends(array, stream_key, low, top_value):
    index_at = [jax.random.randint(jax.random.fold_in(stream_key, axis), (), 0, length) for axis, length in enumerate(array.shape)]
    widest = array.shape.index(max(array.shape))
    neighbour = index_at[:widest] + [(index_at[widest] + 1) % array.shape[widest]] + index_at[widest + 1:]
    return array.at[tuple(index_at)].set(low).at[tuple(neighbour)].set(top_value)


def levels(stream_key, dims, cuts, low, top_value):
    gain, own = 1.0, jax.random.fold_in(stream_key, 6)
    for dim, shards_of in cuts:
        draws = jnp.exp(jax.random.uniform(jax.random.fold_in(own, dim), (shards_of,), jnp.float32, low / len(cuts), top_value / len(cuts)))
        gain = gain * jnp.repeat(draws, dims[dim] // shards_of).reshape([-1 if axis == dim else 1 for axis in range(len(dims))])
    return gain


def noise(key, extent, width, reach, split=(), kind=jnp.bfloat16):
    entries = jax.random.normal(key, extent, jnp.float32) * width
    if len(split) > 0:
        entries = levels(key, extent, split, -0.22, 0.18) * entries
    return jnp.clip(entries, min=-reach, max=reach).astype(kind)


def setup_inputs(seed: int = 0) -> dict:
    splits = jax.random.split(jax.random.key(seed), 9)
    potential = noise(splits[0], (SLICES, R, P_SIZE), 0.5, 3.0, ((0, 4), (2, 8)), jnp.float32)
    direction = noise(splits[1], (SLICES, R, P_SIZE), 1.0, 6.0, ((0, 4), (2, 8)), jnp.float32)
    source = noise(splits[2], (SLICES, R, P_SIZE), 1.0, 6.0, ((0, 4), (2, 8)), jnp.float32)
    region_ids = touch_ends(jax.random.randint(splits[3], (SLICES, R, P_SIZE), 0, NREG), jax.random.fold_in(splits[3], 1), 0, NREG - 1).astype(jnp.int32)
    table_ids = touch_ends(jax.random.randint(splits[4], (SLICES, R, P_SIZE), 0, NTAB), jax.random.fold_in(splits[4], 1), 0, NTAB - 1).astype(jnp.int32)
    region_reluct = jnp.clip(jnp.exp(jax.random.uniform(splits[5], (NREG,), jnp.float32, math.log(0.2), math.log(2.0))), 0.2, 2.0)
    table_sat = jnp.clip(jnp.exp(jax.random.uniform(splits[6], (NTAB,), jnp.float32, math.log(0.05), math.log(1.0))), 0.05, 1.0)
    skew_offsets = touch_ends(jax.random.randint(splits[7], (SLICES,), 0, P_SIZE), jax.random.fold_in(splits[7], 1), 0, P_SIZE - 1).astype(jnp.int32)
    return dict(potential=potential, direction=direction, source=source, region_ids=region_ids, table_ids=table_ids, region_reluct=region_reluct, table_sat=table_sat, skew_offsets=skew_offsets)


GAP_SCALE = 4.0
highest = lax.Precision.HIGHEST


def mode_table(col_start, col_count):
    columns = col_start + jnp.arange(col_count, dtype=jnp.int32)
    mode_ids = jnp.arange(M, dtype=jnp.int32)
    turns = ((2 * mode_ids + 1)[None, :] * (2 * columns + 1)[:, None]) % (4 * P_SIZE)
    phases = turns.astype(jnp.float32) * (math.pi / (2 * P_SIZE))
    return jnp.concatenate([jnp.cos(phases), jnp.sin(phases)], axis=1)


def mode_gains(mode_ids):
    wave = GAP_SCALE * (2 * mode_ids + 1).astype(jnp.float32) / (2 * M)
    return wave / jnp.tanh(wave), wave / jnp.sinh(wave)


def skew_phases(offsets, mode_ids):
    turns = ((2 * mode_ids + 1)[None, :] * offsets[:, None]) % (2 * P_SIZE)
    phases = turns.astype(jnp.float32) * (math.pi / P_SIZE)
    return jnp.cos(phases), jnp.sin(phases)


def couple(harmonics, offsets, mode_ids, axial_total, slice_total):
    self_gain, cross_gain = mode_gains(mode_ids)
    cos_skew, sin_skew = skew_phases(offsets, mode_ids)
    cos_skew = cos_skew[None]
    sin_skew = sin_skew[None]
    rotor = harmonics[:, :, 0]
    stator = harmonics[:, :, 1]
    seen_c = stator[:, :, 0] * cos_skew + stator[:, :, 1] * sin_skew
    seen_s = stator[:, :, 1] * cos_skew - stator[:, :, 0] * sin_skew
    seen = jnp.stack([seen_c, seen_s], axis=2)
    axial = axial_total(jnp.sum(seen, axis=1)) / slice_total
    blended = 0.5 * (seen + axial[:, None])
    rotor_flux = self_gain * rotor - cross_gain * blended
    back = self_gain * seen - cross_gain * rotor
    stator_c = back[:, :, 0] * cos_skew - back[:, :, 1] * sin_skew
    stator_s = back[:, :, 0] * sin_skew + back[:, :, 1] * cos_skew
    stator_flux = jnp.stack([stator_c, stator_s], axis=2)
    return jnp.stack([rotor_flux, stator_flux], axis=2)


def unchanged(total):
    return total


def radial_diff(field, keep):
    inner = field[..., 1:, :] - field[..., :-1, :]
    return jnp.concatenate([inner, -field[..., -1:, :]], axis=-2) * keep


def reluctivity(pot_pad, dir_pad, base, satur, keep):
    pot = pot_pad[..., 1:-1]
    dirv = dir_pad[..., 1:-1]
    rad_p = radial_diff(pot, keep)
    rad_d = radial_diff(dirv, keep)
    azi_p = pot_pad[..., 2:] - pot
    azi_d = dir_pad[..., 2:] - dirv
    square = rad_p * rad_p + azi_p * azi_p
    nu_val = base * (1.0 + satur * square)
    dnu_val = 2.0 * base * satur * (rad_p * rad_d + azi_p * azi_d)
    return nu_val, dnu_val, rad_p, rad_d, azi_p, azi_d


def face_coeff(values, keep):
    inner = 0.5 * (values[..., :-1, :] + values[..., 1:, :])
    return jnp.concatenate([inner, values[..., -1:, :]], axis=-2) * keep


def fluxes(pot_pad, dir_pad, nu_val, dnu_val, nu_pad, dnu_pad, diffs, keep, source):
    rad_p, rad_d, azi_p, azi_d = diffs
    pot = pot_pad[..., 1:-1]
    dirv = dir_pad[..., 1:-1]
    back_p = pot - pot_pad[..., :-2]
    back_d = dirv - dir_pad[..., :-2]
    rad_k = face_coeff(nu_val, keep)
    rad_dk = face_coeff(dnu_val, keep)
    rad_f = rad_k * rad_p
    rad_df = rad_k * rad_d + rad_dk * rad_p
    inner_f = nu_val[..., :1, :] * pot[..., :1, :]
    inner_df = nu_val[..., :1, :] * dirv[..., :1, :] + dnu_val[..., :1, :] * pot[..., :1, :]
    radial = -(rad_f - jnp.concatenate([inner_f, rad_f[..., :-1, :]], axis=-2))
    radial_d = -(rad_df - jnp.concatenate([inner_df, rad_df[..., :-1, :]], axis=-2))
    fwd_k = 0.5 * (nu_val + nu_pad[..., 2:])
    bwd_k = 0.5 * (nu_pad[..., :-2] + nu_val)
    fwd_dk = 0.5 * (dnu_val + dnu_pad[..., 2:])
    bwd_dk = 0.5 * (dnu_pad[..., :-2] + dnu_val)
    azim = -(fwd_k * azi_p - bwd_k * back_p)
    azim_d = -((fwd_k * azi_d + fwd_dk * azi_p) - (bwd_k * back_d + bwd_dk * back_p))
    return radial + azim - source, radial_d + azim_d


def reference(potential, direction, source, region_ids, table_ids, region_reluct, table_sat, skew_offsets):
    keep = (jnp.arange(R) != RG - 1).astype(jnp.float32)[:, None]
    table = mode_table(0, P_SIZE)
    fields = jnp.stack([potential[:, RG - 1:RG + 1, :], direction[:, RG - 1:RG + 1, :]])
    harmonics = jnp.dot(fields.reshape(-1, P_SIZE), table, precision=highest).reshape(2, SLICES, 2, 2, M)
    mode_ids = jnp.arange(M, dtype=jnp.int32)
    coupled = couple(harmonics, skew_offsets, mode_ids, unchanged, SLICES)
    gap_flux = (jnp.dot(coupled.reshape(-1, 2 * M), table.T, precision=highest) * (2.0 / P_SIZE)).reshape(2, SLICES, 2, P_SIZE)

    def one_slice(items):
        pot, dirv, src, regions, tables, flux_pot, flux_dir = items
        base = region_reluct[regions]
        satur = table_sat[tables]
        pot_pad = jnp.concatenate([-pot[:, -1:], pot, -pot[:, :1]], axis=-1)
        dir_pad = jnp.concatenate([-dirv[:, -1:], dirv, -dirv[:, :1]], axis=-1)
        nu_val, dnu_val, rad_p, rad_d, azi_p, azi_d = reluctivity(pot_pad, dir_pad, base, satur, keep)
        nu_pad = jnp.concatenate([nu_val[:, -1:], nu_val, nu_val[:, :1]], axis=-1)
        dnu_pad = jnp.concatenate([dnu_val[:, -1:], dnu_val, dnu_val[:, :1]], axis=-1)
        res_part, jac_part = fluxes(pot_pad, dir_pad, nu_val, dnu_val, nu_pad, dnu_pad, (rad_p, rad_d, azi_p, azi_d), keep, src)
        res_part = res_part.at[RG - 1:RG + 1, :].add(flux_pot)
        jac_part = jac_part.at[RG - 1:RG + 1, :].add(flux_dir)
        return res_part, jac_part

    residual, jac_product = lax.map(one_slice, (potential, direction, source, region_ids, table_ids, gap_flux[0], gap_flux[1]))
    return (residual, jac_product, gap_flux)
```

```python
import functools
import math

import jax
import jax.numpy as jnp
import numpy as np
from jax import lax
from jax.experimental import pallas as pl
from jax.experimental.pallas import tpu as pltpu
from jax.sharding import PartitionSpec as P

NREG = 8
NTAB = 16
RG = 512
GAP_SCALE = 4.0
LANES = 128
highest = lax.Precision.HIGHEST


def transform_tables(period):
    ka = period // (2 * LANES)
    a = np.arange(ka)
    b = np.arange(LANES)
    first = np.exp(-2j * np.pi * np.outer(a, a) / ka - 1j * np.pi * a[None, :] * LANES / period)
    w1 = np.block([[first.real, first.imag], [first.imag, -first.real]])
    twiddle = np.exp(
        -2j * np.pi * np.outer(a, b) / (ka * LANES) - 1j * np.pi * b[None, :] / period
    )
    second = np.exp(-2j * np.pi * np.outer(b, b) / LANES)
    w2 = np.block([[second.real, second.imag], [-second.imag, second.real]])
    back2 = np.conj(second)
    w2i = np.block([[back2.real, back2.imag], [-back2.imag, back2.real]])
    back1 = np.conj(first).T / (ka * LANES)
    w1i = np.block([[back1.real, -back1.imag], [-back1.imag, -back1.real]])
    freq = (4 * (a[:, None] + ka * b[None, :]) + 1) % (2 * period)
    odd = np.minimum(freq, 2 * period - freq)
    wave = GAP_SCALE * odd / period
    gains = np.stack([wave / np.tanh(wave), wave / np.sinh(wave)])
    twiddles = np.stack([twiddle.real, twiddle.imag])
    return [np.asarray(t, np.float32) for t in (w1, twiddles, w2, w2i, w1i, gains)]


def edge_kernel(
    off_ref, af, al, vf, vl, rf, rl, tf, tl, a0, a1, v0, v1, left_ref, right_ref, rows_ref
):
    s = pl.program_id(0)
    rows = af.shape[1]
    lane = lax.broadcasted_iota(jnp.int32, (LANES, LANES), 1)
    last = LANES - 1

    def pick(mix, ref, at, source, target):
        tile = ref[0, pl.ds(at, LANES), :].astype(jnp.float32)
        shift = (target - source) % LANES
        if shift:
            tile = pltpu.roll(tile, shift, 1)
        return jnp.where(lane == target, tile, mix)

    for block in range(rows // LANES):
        at = block * LANES
        mix = jnp.zeros((LANES, LANES), jnp.float32)
        tile = af[0, pl.ds(at, LANES), :]
        mix = jnp.where(lane < 2, tile, mix)
        tile = pltpu.roll(vf[0, pl.ds(at, LANES), :], 2, 1)
        mix = jnp.where((lane >= 2) & (lane < 4), tile, mix)
        mix = pick(mix, rf, at, 0, 4)
        mix = pick(mix, tf, at, 0, 5)
        mix = pick(mix, al, at, last, 8)
        mix = pick(mix, vl, at, last, 9)
        mix = pick(mix, rl, at, last, 10)
        mix = pick(mix, tl, at, last, 11)
        flat = jnp.transpose(mix)
        left_ref[0, :, pl.ds(at, LANES)] = flat[0:8]
        right_ref[0, :, pl.ds(at, LANES)] = flat[8:16]
    count = rows_ref.shape[2]
    for c in range(count):
        cut = pl.ds(c * LANES, LANES)
        rows_ref[0, 0, c : c + 1, :] = a0[0, 7:8, cut]
        rows_ref[0, 1, c : c + 1, :] = a1[0, 0:1, cut]
        rows_ref[0, 2, c : c + 1, :] = v0[0, 7:8, cut]
        rows_ref[0, 3, c : c + 1, :] = v1[0, 0:1, cut]
        rows_ref[0, 4, c : c + 1, :] = jnp.full((1, LANES), off_ref[s], jnp.int32).astype(
            jnp.float32
        )


def edges(potential, direction, regions, tables, offsets):
    slices, rows, width = potential.shape
    count = width // LANES
    first = pl.BlockSpec((1, rows, LANES), lambda s: (s, 0, 0))
    last = pl.BlockSpec((1, rows, LANES), lambda s: (s, 0, count - 1))
    rotor = pl.BlockSpec((1, 8, width), lambda s: (s, RG // 8 - 1, 0))
    stator = pl.BlockSpec((1, 8, width), lambda s: (s, RG // 8, 0))
    return pl.pallas_call(
        edge_kernel,
        grid=(slices,),
        in_specs=[pl.BlockSpec(memory_space=pltpu.SMEM)]
        + [first, last] * 4
        + [rotor, stator] * 2,
        out_specs=[
            pl.BlockSpec((1, 8, rows), lambda s: (s, 0, 0)),
            pl.BlockSpec((1, 8, rows), lambda s: (s, 0, 0)),
            pl.BlockSpec((1, 5, count, LANES), lambda s: (s, 0, 0, 0)),
        ],
        out_shape=[
            jax.ShapeDtypeStruct((slices, 8, rows), jnp.float32),
            jax.ShapeDtypeStruct((slices, 8, rows), jnp.float32),
            jax.ShapeDtypeStruct((slices, 5, count, LANES), jnp.float32),
        ],
        compiler_params=pltpu.CompilerParams(vmem_limit_bytes=32 * 2**20),
        cost_estimate=pl.CostEstimate(
            flops=slices * rows * 1000, bytes_accessed=slices * rows * 4096, transcendentals=0
        ),
    )(
        offsets,
        potential,
        potential,
        direction,
        direction,
        regions,
        regions,
        tables,
        tables,
        potential,
        potential,
        direction,
        direction,
    )


def stencil_kernel(
    reg_s,
    tab_s,
    sign_s,
    regv,
    tabv,
    own_ref,
    low_ref,
    high_ref,
    a_ref,
    v_ref,
    src_ref,
    r_ref,
    t_ref,
    ax,
    vx,
    rx,
    tx,
    res_ref,
    jac_ref,
    halo,
    carry_ref,
):
    block = pl.program_id(1)
    blocks = pl.num_programs(1)
    size = a_ref.shape[1]
    count = a_ref.shape[2] // LANES
    rows = own_ref.shape[2]
    tiles = size // 8
    shape = (8, LANES)
    lane = lax.broadcasted_iota(jnp.int32, shape, 1)
    row = lax.broadcasted_iota(jnp.int32, shape, 0)
    at_end = lane == LANES - 1
    at_start = lane == 0
    at_bottom = row == 7
    at_top = row == 0
    reg_tab = jnp.broadcast_to(regv[0:1, :], shape)
    sat_tab = jnp.broadcast_to(tabv[0:1, :], shape)

    @pl.when(block == 0)
    def _():
        col = lax.broadcasted_iota(jnp.int32, (1, rows), 1)

        def pick(ids, table, number):
            total = jnp.zeros_like(ids)
            for i in range(number):
                total = jnp.where(ids == float(i), table[i], total)
            return total

        def material(a, a_next, v, v_next, reg, tab):
            def radial(x):
                follow = jnp.where(col == rows - 1, 0.0, pltpu.roll(x, rows - 1, 1))
                return jnp.where(col == RG - 1, 0.0, follow - x)

            base = pick(reg, reg_s, NREG)
            satur = pick(tab, tab_s, NTAB)
            rp, rd = radial(a), radial(v)
            zp, zd = a_next - a, v_next - v
            nu = base * (1.0 + satur * (rp * rp + zp * zp))
            dnu = 2.0 * base * satur * (rp * rd + zp * zd)
            return nu, dnu, zp, zd

        own = [own_ref[0, i : i + 1, :] for i in range(6)]
        high = [high_ref[0, i : i + 1, :] for i in range(6)]
        low = [low_ref[0, i : i + 1, :] for i in range(4)]
        ls, rs = sign_s[0], sign_s[1]
        high = [x * rs for x in high[:4]] + high[4:]
        low = [x * ls for x in low[:2]] + low[2:]
        nu0, dnu0, _, _ = material(*own)
        nur, dnur, _, _ = material(*high)
        nul, dnul, zp, zd = material(low[0], own[0], low[1], own[2], low[2], low[3])
        k = 0.5 * (nul + nu0)
        dk = 0.5 * (dnul + dnu0)
        flux = k * zp
        dflux = k * zd + dk * zp
        pack = jnp.concatenate(
            [flux, dflux, dflux, dflux, high[0], high[2], nur, dnur], axis=0
        )
        for i in range(rows // LANES):
            piece = jnp.concatenate(
                [
                    jnp.broadcast_to(pack[0:1, i * LANES : (i + 1) * LANES], (LANES - 8, LANES)),
                    pack[:, i * LANES : (i + 1) * LANES],
                ],
                axis=0,
            )
            halo[i * LANES : (i + 1) * LANES, :] = jnp.transpose(piece)


    def load(ref, at):
        return [ref[0, pl.ds(at, 8), c * LANES : (c + 1) * LANES] for c in range(count)]

    def up(x, follow):
        return [
            jnp.where(at_bottom, pltpu.roll(y, 7, 0), pltpu.roll(z, 7, 0))
            for z, y in zip(x, follow)
        ]

    def down(x, before):
        return [
            jnp.where(at_top, pltpu.roll(y, 1, 0), pltpu.roll(z, 1, 0))
            for z, y in zip(x, before)
        ]

    def forward(x, end):
        turned = [pltpu.roll(z, LANES - 1, 1) for z in x]
        return [
            jnp.where(at_end, turned[c + 1] if c + 1 < count else end, turned[c])
            for c in range(count)
        ]

    def backward(x, start):
        turned = [pltpu.roll(z, 1, 1) for z in x]
        return [jnp.where(at_start, turned[c - 1] if c else start, turned[c]) for c in range(count)]

    def each(f, *xs):
        return [f(*x) for x in zip(*xs)]

    def material(a, v, a_down, v_down, reg, tab, h):
        rp = each(lambda x, y: y - x, a, a_down)
        rd = each(lambda x, y: y - x, v, v_down)
        zp = each(lambda x, y: y - x, a, forward(a, pltpu.roll(h, 3, 1)))
        zd = each(lambda x, y: y - x, v, forward(v, pltpu.roll(h, 2, 1)))

        def coefficients(rp, rd, zp, zd, reg, tab):
            base = jnp.take_along_axis(reg_tab, reg, axis=1, mode="promise_in_bounds")
            satur = jnp.take_along_axis(sat_tab, tab, axis=1, mode="promise_in_bounds")
            bs = base * satur
            return (
                0.5 * (base + bs * (rp * rp + zp * zp)),
                bs * (rp * rd + zp * zd),
            )

        both = each(coefficients, rp, rd, zp, zd, reg, tab)
        return [x[0] for x in both], [x[1] for x in both], rp, rd, zp, zd

    start_row = block * size

    def halo_at(at):
        return halo[pl.ds(pl.multiple_of(start_row + at, 8), 8), :]

    def emit(at, cur, h, nu_next, dnu_next, fr_before, dfr_before):
        nu, dnu, rp, rd, zp, zd = cur
        kr = each(lambda x, y: x + y, nu, up(nu, nu_next))
        dkr = each(lambda x, y: x + y, dnu, up(dnu, dnu_next))
        fr = each(lambda x, y: x * y, kr, rp)
        dfr = each(lambda k, d, dk, p: k * d + dk * p, kr, rd, dkr, rp)
        half = 0.5
        kf = each(lambda x, y: x + y, nu, forward(nu, half * pltpu.roll(h, 1, 1)))
        dkf = each(lambda x, y: x + y, dnu, forward(dnu, half * h))
        fz = each(lambda x, y: x * y, kf, zp)
        dfz = each(lambda k, d, dk, p: k * d + dk * p, kf, zd, dkf, zp)
        fr_up = down(fr, fr_before)
        dfr_up = down(dfr, dfr_before)
        fz_back = backward(fz, h)
        dfz_back = backward(dfz, pltpu.roll(h, LANES - 121, 1))
        for c in range(count):
            cut = slice(c * LANES, (c + 1) * LANES)
            where = (0, pl.ds(at, 8), cut)
            res_ref[where] = (fr_up[c] - fr[c]) + (fz_back[c] - fz[c]) - src_ref[where]
            jac_ref[where] = (dfr_up[c] - dfr[c]) + (dfz_back[c] - dfz[c])
        return fr, dfr

    def tile_material(at, a_after, v_after):
        a, v = load(a_ref, at), load(v_ref, at)
        h = halo_at(at)
        return material(
            a, v, up(a, a_after), up(v, v_after), load(r_ref, at), load(t_ref, at), h
        )

    cur = tile_material(0, load(a_ref, 8), load(v_ref, 8))

    @pl.when(block == 0)
    def _():
        a, v = load(a_ref, 0), load(v_ref, 0)
        for c in range(count):
            cut = slice(c * LANES, (c + 1) * LANES)
            inner = 2.0 * cur[0][c] * a[c]
            dinner = 2.0 * cur[0][c] * v[c] + 2.0 * cur[1][c] * a[c]
            carry_ref[0, :, cut] = pltpu.roll(inner, 7, 0)
            carry_ref[1, :, cut] = pltpu.roll(dinner, 7, 0)

    fr = [carry_ref[0, :, c * LANES : (c + 1) * LANES] for c in range(count)]
    dfr = [carry_ref[1, :, c * LANES : (c + 1) * LANES] for c in range(count)]

    def step(t, state):
        cur, fr, dfr = state
        at = pl.multiple_of(t * 8, 8)
        after = pl.multiple_of(t * 8 + 8, 8)
        beyond = pl.multiple_of(t * 8 + 16, 8)
        following = tile_material(after, load(a_ref, beyond), load(v_ref, beyond))
        fr, dfr = emit(at, cur, halo_at(at), following[0], following[1], fr, dfr)
        return following, fr, dfr

    cur, fr, dfr = lax.fori_loop(0, tiles - 2, step, (cur, fr, dfr))

    is_last = block == blocks - 1
    is_gap = start_row + size == RG
    end = size - 8

    def ending(ref, ext):
        own, beyond = load(ref, end), load(ext, 0)
        return each(
            lambda x, y: jnp.where(is_gap, pltpu.roll(x, 1, 0), jnp.where(is_last, 0.0, y)),
            own,
            beyond,
        )

    following = tile_material(end, ending(a_ref, ax), ending(v_ref, vx))
    fr, dfr = emit(end - 8, cur, halo_at(end - 8), following[0], following[1], fr, dfr)
    cur = following
    a, v = load(ax, 0), load(vx, 0)
    h = halo[pl.ds(pl.multiple_of(jnp.minimum(start_row + size, rows - 8), 8), 8), :]
    beyond = material(a, v, up(a, a), up(v, v), load(rx, 0), load(tx, 0), h)
    nu_next = each(lambda x, y: jnp.where(is_last, pltpu.roll(x, 1, 0), y), cur[0], beyond[0])
    dnu_next = each(lambda x, y: jnp.where(is_last, pltpu.roll(x, 1, 0), y), cur[1], beyond[1])
    fr, dfr = emit(end, cur, halo_at(end), nu_next, dnu_next, fr, dfr)
    for c in range(count):
        cut = slice(c * LANES, (c + 1) * LANES)
        carry_ref[0, :, cut] = fr[c]
        carry_ref[1, :, cut] = dfr[c]


BLOCK = 256


def stencil(potential, direction, source, regions, tables, reg, sat, signs, own, low, high):
    slices, rows, width = potential.shape
    blocks = rows // BLOCK
    whole = pl.BlockSpec((1, BLOCK, width), lambda s, i: (s, i, 0))
    after = pl.BlockSpec(
        (1, 8, width),
        lambda s, i: (s, jnp.minimum((i + 1) * (BLOCK // 8), rows // 8 - 1), 0),
    )
    edge = pl.BlockSpec((1, 8, rows), lambda s, i: (s, 0, 0))
    table = pl.BlockSpec((8, LANES), lambda s, i: (0, 0))
    smem = pl.BlockSpec(memory_space=pltpu.SMEM)
    regv = jnp.broadcast_to(jnp.pad(reg, (0, LANES - NREG)), (8, LANES))
    tabv = jnp.broadcast_to(jnp.pad(sat, (0, LANES - NTAB)), (8, LANES))
    return pl.pallas_call(
        stencil_kernel,
        grid=(slices, blocks),
        in_specs=[smem] * 3 + [table] * 2 + [edge] * 3 + [whole] * 5 + [after] * 4,
        out_specs=[whole, whole],
        out_shape=[jax.ShapeDtypeStruct(potential.shape, jnp.float32)] * 2,
        scratch_shapes=[
            pltpu.VMEM((rows, LANES), jnp.float32),
            pltpu.VMEM((2, 8, width), jnp.float32),
        ],
        compiler_params=pltpu.CompilerParams(vmem_limit_bytes=32 * 2**20),
        cost_estimate=pl.CostEstimate(
            flops=slices * rows * width * 60,
            bytes_accessed=slices * rows * width * 28,
            transcendentals=0,
        ),
    )(
        reg,
        sat,
        signs,
        regv,
        tabv,
        own,
        low,
        high,
        potential,
        direction,
        source,
        regions,
        tables,
        potential,
        direction,
        regions,
        tables,
    )


def gap_kernel(
    azims, mine, rows_ref, w1, tw, w2, w2i, w1i, gains, res_in, jac_in, res_ref, jac_ref, gap_ref,
    grid_z, grid_u, seen_ref,
):
    step = pl.program_id(0)
    devices, slices, _, count, _ = rows_ref.shape
    total = devices // azims * slices
    ka = tw.shape[1]
    own = mine[0]

    def dot(x, y):
        return jnp.dot(x, y, precision=highest, preferred_element_type=jnp.float32)

    @pl.when(step == 0)
    def _():
        owned = 2 * slices
        vectors = owned + 2 * total

        def gather(v, cut, s, q):
            for a in range(azims):
                grid_z[a * count : (a + 1) * count, v * LANES : (v + 1) * LANES] = rows_ref[
                    cut * azims + a, s, q
                ]

        for f in range(2):
            for s in range(slices):
                gather(f * slices + s, own, s, 2 * f)
            for s in range(total):
                gather(owned + f * total + s, s // slices, s % slices, 2 * f + 1)
        first = dot(w1[...], grid_z[...])
        tr, ti = tw[0], tw[1]
        for v in range(vectors):
            re = first[0:ka, v * LANES : (v + 1) * LANES]
            im = first[ka : 2 * ka, v * LANES : (v + 1) * LANES]
            grid_u[v * ka : (v + 1) * ka, 0:LANES] = re * tr - im * ti
            grid_u[v * ka : (v + 1) * ka, LANES : 2 * LANES] = re * ti + im * tr
        bins = dot(grid_u[...], w2[...])

        def part(v):
            return (
                bins[v * ka : (v + 1) * ka, 0:LANES],
                bins[v * ka : (v + 1) * ka, LANES : 2 * LANES],
            )

        k1 = lax.broadcasted_iota(jnp.int32, (ka, LANES), 0)
        k2 = lax.broadcasted_iota(jnp.int32, (ka, LANES), 1)
        freq = 4 * k1 + 4 * ka * k2 + 1
        period = 2 * ka * LANES

        def skew(cut, s):
            offset = jnp.broadcast_to(
                rows_ref[cut * azims, s, 4, 0:1, :].astype(jnp.int32), (ka, LANES)
            )
            angle = (freq * offset & (2 * period - 1)).astype(jnp.float32) * (math.pi / period)
            return jnp.cos(angle), jnp.sin(angle)

        axial = [[0.0, 0.0], [0.0, 0.0]]
        for s in range(total):
            c, d = skew(s // slices, s % slices)
            for f in range(2):
                re, im = part(owned + f * total + s)
                x, y = re * c - im * d, re * d + im * c
                seen_ref[s, f, 0] = x
                seen_ref[s, f, 1] = y
                axial[f][0] = axial[f][0] + x
                axial[f][1] = axial[f][1] + y
        self_gain, cross_gain = gains[0], gains[1]
        for s in range(slices):
            c, d = skew(own, s)
            for f in range(2):
                seen = [seen_ref[own * slices + s, f, i] for i in range(2)]
                rotor = part(f * slices + s)
                blended = [0.5 * (seen[i] + axial[f][i] * (1.0 / total)) for i in range(2)]
                flux = [self_gain * rotor[i] - cross_gain * blended[i] for i in range(2)]
                back = [self_gain * seen[i] - cross_gain * rotor[i] for i in range(2)]
                stator = (back[0] * c + back[1] * d, back[1] * c - back[0] * d)
                for r, value in enumerate((flux, stator)):
                    v = (f * slices + s) * 2 + r
                    grid_u[v * ka : (v + 1) * ka, 0:LANES] = value[0]
                    grid_u[v * ka : (v + 1) * ka, LANES : 2 * LANES] = value[1]
        outs = 4 * slices
        lines = dot(grid_u[0 : outs * ka, :], w2i[...])
        for v in range(outs):
            re = lines[v * ka : (v + 1) * ka, 0:LANES]
            im = lines[v * ka : (v + 1) * ka, LANES : 2 * LANES]
            grid_z[0:ka, v * LANES : (v + 1) * LANES] = re * tr + im * ti
            grid_z[ka : 2 * ka, v * LANES : (v + 1) * LANES] = im * tr - re * ti
        last = dot(w1i[...], grid_z[:, 0 : outs * LANES])
        for f in range(2):
            for s in range(slices):
                for r in range(2):
                    v = (f * slices + s) * 2 + r
                    for c in range(count):
                        gap_ref[f, s, r : r + 1, c * LANES : (c + 1) * LANES] = last[
                            c : c + 1, v * LANES : (v + 1) * LANES
                        ]

    width = res_in.shape[2]
    line = lax.broadcasted_iota(jnp.int32, (8, width), 0)
    for s in range(slices):
        for f, (old, new) in enumerate(((res_in, res_ref), (jac_in, jac_ref))):
            pair = gap_ref[f, s]
            add = jnp.where(step == 0, pair[0:1], pair[1:2])
            target = jnp.where(step == 0, 7, 0)
            new[s] = jnp.where(line == target, old[s] + add, old[s])


def gap(residual, jac_product, gathered, azims, mine, position):
    slices, rows, width = residual.shape
    devices = gathered.shape[0]
    count = width // LANES
    period = azims * width
    ka = period // (2 * LANES)
    w1, tw, w2, w2i, w1i, gains = transform_tables(period)
    lines = -(-count // 8) * 8
    w1i = np.pad(w1i, ((0, lines), (0, 0)))
    mine_w1i = lax.dynamic_slice_in_dim(jnp.asarray(w1i), position * count, lines, 0)
    total = devices // azims * slices
    vectors = 2 * slices + 2 * total
    touched = pl.BlockSpec((slices, 8, width), lambda g: (0, RG // 8 - 1 + g, 0))

    def full(x):
        zeros = (0,) * len(x.shape)
        return pl.BlockSpec(x.shape, lambda g: zeros)

    operands = [gathered] + [jnp.asarray(x) for x in (w1, tw, w2, w2i)]
    operands += [mine_w1i, jnp.asarray(gains)]
    shape = (2, slices, 2, width)
    return pl.pallas_call(
        functools.partial(gap_kernel, azims),
        grid=(2,),
        in_specs=[pl.BlockSpec(memory_space=pltpu.SMEM)]
        + [full(x) for x in operands]
        + [touched, touched],
        out_specs=[touched, touched, pl.BlockSpec(shape, lambda g: (0, 0, 0, 0))],
        out_shape=[
            jax.ShapeDtypeStruct(residual.shape, jnp.float32),
            jax.ShapeDtypeStruct(residual.shape, jnp.float32),
            jax.ShapeDtypeStruct(shape, jnp.float32),
        ],
        scratch_shapes=[
            pltpu.VMEM((2 * ka, vectors * LANES), jnp.float32),
            pltpu.VMEM((vectors * ka, 2 * LANES), jnp.float32),
            pltpu.VMEM((total, 2, 2, ka, LANES), jnp.float32),
        ],
        input_output_aliases={8: 0, 9: 1},
        compiler_params=pltpu.CompilerParams(vmem_limit_bytes=32 * 2**20),
        cost_estimate=pl.CostEstimate(
            flops=vectors * ka * 2 * LANES * 1000, bytes_accessed=2**21, transcendentals=0
        ),
    )(mine, *operands, residual, jac_product)


def body(
    potential, direction, source, region_ids, table_ids, region_reluct, table_sat, skew_offsets
):
    position = lax.axis_index("azim")
    azims = lax.axis_size("azim")
    left, right, rows = edges(potential, direction, region_ids, table_ids, skew_offsets)
    forward = [(i, (i + 1) % azims) for i in range(azims)]
    backward = [(target, source_) for source_, target in forward]
    low = lax.ppermute(right, "azim", forward)
    high = lax.ppermute(left, "azim", backward)
    gathered = lax.all_gather(rows, ("cuts", "azim"))
    signs = jnp.stack(
        [jnp.where(position == 0, -1.0, 1.0), jnp.where(position == azims - 1, -1.0, 1.0)]
    ).astype(jnp.float32)
    residual, jac_product = stencil(
        potential,
        direction,
        source,
        region_ids,
        table_ids,
        region_reluct,
        table_sat,
        signs,
        left,
        low,
        high,
    )
    mine = lax.axis_index("cuts").astype(jnp.int32).reshape(1)
    return tuple(gap(residual, jac_product, gathered, azims, mine, position))


def solution(mesh):
    return jax.shard_map(
        body,
        mesh=mesh,
        in_specs=(
            P("cuts", None, "azim"),
            P("cuts", None, "azim"),
            P("cuts", None, "azim"),
            P("cuts", None, "azim"),
            P("cuts", None, "azim"),
            P(),
            P(),
            P("cuts"),
        ),
        out_specs=(P("cuts", None, "azim"), P("cuts", None, "azim"), P(None, "cuts", None, "azim")),
        check_vma=False,
    )
```

```python
import functools
import math

import jax
import jax.numpy as jnp
import numpy as np
from jax import lax
from jax.experimental import pallas as pl
from jax.experimental.pallas import tpu as pltpu
from jax.sharding import PartitionSpec as P

NREG = 8
NTAB = 16
RG = 512
GAP_SCALE = 4.0
LANES = 128
highest = lax.Precision.HIGHEST


def transform_tables(period):
    ka = period // (2 * LANES)
    a = np.arange(ka)
    b = np.arange(LANES)
    first = np.exp(-2j * np.pi * np.outer(a, a) / ka - 1j * np.pi * a[None, :] * LANES / period)
    w1 = np.block([[first.real, first.imag], [first.imag, -first.real]])
    twiddle = np.exp(
        -2j * np.pi * np.outer(a, b) / (ka * LANES) - 1j * np.pi * b[None, :] / period
    )
    second = np.exp(-2j * np.pi * np.outer(b, b) / LANES)
    w2 = np.block([[second.real, second.imag], [-second.imag, second.real]])
    back2 = np.conj(second)
    w2i = np.block([[back2.real, back2.imag], [-back2.imag, back2.real]])
    back1 = np.conj(first).T / (ka * LANES)
    w1i = np.block([[back1.real, -back1.imag], [-back1.imag, -back1.real]])
    freq = (4 * (a[:, None] + ka * b[None, :]) + 1) % (2 * period)
    odd = np.minimum(freq, 2 * period - freq)
    wave = GAP_SCALE * odd / period
    gains = np.stack([wave / np.tanh(wave), wave / np.sinh(wave)])
    twiddles = np.stack([twiddle.real, twiddle.imag])
    return [np.asarray(t, np.float32) for t in (w1, twiddles, w2, w2i, w1i, gains)]


def edge_kernel(
    off_ref, af, al, vf, vl, rf, rl, tf, tl, a0, a1, v0, v1, left_ref, right_ref, rows_ref
):
    s = pl.program_id(0)
    rows = af.shape[1]
    lane = lax.broadcasted_iota(jnp.int32, (LANES, LANES), 1)
    last = LANES - 1

    def pick(mix, ref, at, source, target):
        tile = ref[0, pl.ds(at, LANES), :].astype(jnp.float32)
        shift = (target - source) % LANES
        if shift:
            tile = pltpu.roll(tile, shift, 1)
        return jnp.where(lane == target, tile, mix)

    for block in range(rows // LANES):
        at = block * LANES
        mix = jnp.zeros((LANES, LANES), jnp.float32)
        tile = af[0, pl.ds(at, LANES), :]
        mix = jnp.where(lane < 2, tile, mix)
        tile = pltpu.roll(vf[0, pl.ds(at, LANES), :], 2, 1)
        mix = jnp.where((lane >= 2) & (lane < 4), tile, mix)
        mix = pick(mix, rf, at, 0, 4)
        mix = pick(mix, tf, at, 0, 5)
        mix = pick(mix, al, at, last, 8)
        mix = pick(mix, vl, at, last, 9)
        mix = pick(mix, rl, at, last, 10)
        mix = pick(mix, tl, at, last, 11)
        flat = jnp.transpose(mix)
        left_ref[0, :, pl.ds(at, LANES)] = flat[0:8]
        right_ref[0, :, pl.ds(at, LANES)] = flat[8:16]
    count = rows_ref.shape[2]
    for c in range(count):
        cut = pl.ds(c * LANES, LANES)
        rows_ref[0, 0, c : c + 1, :] = a0[0, 7:8, cut]
        rows_ref[0, 1, c : c + 1, :] = a1[0, 0:1, cut]
        rows_ref[0, 2, c : c + 1, :] = v0[0, 7:8, cut]
        rows_ref[0, 3, c : c + 1, :] = v1[0, 0:1, cut]
        rows_ref[0, 4, c : c + 1, :] = jnp.full((1, LANES), off_ref[s], jnp.int32).astype(
            jnp.float32
        )


def edges(potential, direction, regions, tables, offsets):
    slices, rows, width = potential.shape
    count = width // LANES
    first = pl.BlockSpec((1, rows, LANES), lambda s: (s, 0, 0))
    last = pl.BlockSpec((1, rows, LANES), lambda s: (s, 0, count - 1))
    rotor = pl.BlockSpec((1, 8, width), lambda s: (s, RG // 8 - 1, 0))
    stator = pl.BlockSpec((1, 8, width), lambda s: (s, RG // 8, 0))
    return pl.pallas_call(
        edge_kernel,
        grid=(slices,),
        in_specs=[pl.BlockSpec(memory_space=pltpu.SMEM)]
        + [first, last] * 4
        + [rotor, stator] * 2,
        out_specs=[
            pl.BlockSpec((1, 8, rows), lambda s: (s, 0, 0)),
            pl.BlockSpec((1, 8, rows), lambda s: (s, 0, 0)),
            pl.BlockSpec((1, 5, count, LANES), lambda s: (s, 0, 0, 0)),
        ],
        out_shape=[
            jax.ShapeDtypeStruct((slices, 8, rows), jnp.float32),
            jax.ShapeDtypeStruct((slices, 8, rows), jnp.float32),
            jax.ShapeDtypeStruct((slices, 5, count, LANES), jnp.float32),
        ],
        compiler_params=pltpu.CompilerParams(vmem_limit_bytes=58 * 2**20),
        cost_estimate=pl.CostEstimate(
            flops=slices * rows * 1000, bytes_accessed=slices * rows * 4096, transcendentals=0
        ),
    )(
        offsets,
        potential,
        potential,
        direction,
        direction,
        regions,
        regions,
        tables,
        tables,
        potential,
        potential,
        direction,
        direction,
    )


def exchange_kernel(
    azims, cuts, left, right, rows, low, high, gathered, edge_send, edge_recv, azim_send, azim_recv,
    cut_send, cut_recv,
):
    pos = lax.axis_index("azim")
    cut = lax.axis_index("cuts")
    mesh_id = pl.DeviceIdType.MESH

    def along(axis, here, number, k):
        return {axis: lax.rem(here + k, number)}

    peers = [along("azim", pos, azims, k) for k in range(1, azims)]
    others = [along("cuts", cut, cuts, k) for k in range(1, cuts)]
    barrier = pltpu.get_barrier_semaphore()
    for peer in peers + others:
        pl.semaphore_signal(barrier, inc=1, device_id=peer, device_id_type=mesh_id)
    pl.semaphore_wait(barrier, len(peers) + len(others))

    def send(src, dst, send_sem, recv_sem, peer):
        copy = pltpu.make_async_remote_copy(
            src_ref=src,
            dst_ref=dst,
            send_sem=send_sem,
            recv_sem=recv_sem,
            device_id=peer,
            device_id_type=mesh_id,
        )
        copy.start()
        return copy

    slot = gathered.at[cut, pos]
    inner = [
        send(rows, slot, azim_send.at[k], azim_recv.at[k], peer) for k, peer in enumerate(peers)
    ]
    borders = [
        send(right, low, edge_send.at[0], edge_recv.at[0], along("azim", pos, azims, 1)),
        send(left, high, edge_send.at[1], edge_recv.at[1], along("azim", pos, azims, azims - 1)),
    ]
    gathered[cut, pos] = rows[...]
    for copy in inner:
        copy.wait()
    outer = [
        send(gathered.at[cut], gathered.at[cut], cut_send.at[k], cut_recv.at[k], peer)
        for k, peer in enumerate(others)
    ]
    for copy in borders + outer:
        copy.wait()


def exchange(left, right, rows):
    azims, cuts = lax.axis_size("azim"), lax.axis_size("cuts")
    vmem = pl.BlockSpec(memory_space=pltpu.VMEM)
    dma = pltpu.SemaphoreType.DMA
    return pl.pallas_call(
        functools.partial(exchange_kernel, azims, cuts),
        in_specs=[vmem] * 3,
        out_specs=[vmem] * 3,
        out_shape=[
            jax.ShapeDtypeStruct(left.shape, jnp.float32),
            jax.ShapeDtypeStruct(left.shape, jnp.float32),
            jax.ShapeDtypeStruct((cuts, azims) + rows.shape, jnp.float32),
        ],
        scratch_shapes=[dma((2,))] * 2 + [dma((azims - 1,))] * 2 + [dma((cuts - 1,))] * 2,
        compiler_params=pltpu.CompilerParams(
            collective_id=0, has_side_effects=True, vmem_limit_bytes=58 * 2**20
        ),
    )(left, right, rows)


def stencil_kernel(
    reg_s,
    tab_s,
    sign_s,
    regv,
    tabv,
    own_ref,
    low_ref,
    high_ref,
    a_ref,
    v_ref,
    src_ref,
    r_ref,
    t_ref,
    ax,
    vx,
    rx,
    tx,
    res_ref,
    jac_ref,
    halo,
    carry_ref,
):
    block = pl.program_id(1)
    blocks = pl.num_programs(1)
    size = a_ref.shape[1]
    count = a_ref.shape[2] // LANES
    rows = own_ref.shape[2]
    tiles = size // 8
    shape = (8, LANES)
    lane = lax.broadcasted_iota(jnp.int32, shape, 1)
    row = lax.broadcasted_iota(jnp.int32, shape, 0)
    at_end = lane == LANES - 1
    at_start = lane == 0
    at_bottom = row == 7
    at_top = row == 0
    reg_tab = jnp.broadcast_to(regv[0:1, :], shape)
    sat_tab = jnp.broadcast_to(tabv[0:1, :], shape)

    @pl.when(block == 0)
    def _():
        col = lax.broadcasted_iota(jnp.int32, (1, rows), 1)

        def pick(ids, table, number):
            total = jnp.zeros_like(ids)
            for i in range(number):
                total = jnp.where(ids == float(i), table[i], total)
            return total

        def material(a, a_next, v, v_next, reg, tab):
            def radial(x):
                follow = jnp.where(col == rows - 1, 0.0, pltpu.roll(x, rows - 1, 1))
                return jnp.where(col == RG - 1, 0.0, follow - x)

            base = pick(reg, reg_s, NREG)
            satur = pick(tab, tab_s, NTAB)
            rp, rd = radial(a), radial(v)
            zp, zd = a_next - a, v_next - v
            nu = base * (1.0 + satur * (rp * rp + zp * zp))
            dnu = 2.0 * base * satur * (rp * rd + zp * zd)
            return nu, dnu, zp, zd

        own = [own_ref[0, i : i + 1, :] for i in range(6)]
        high = [high_ref[0, i : i + 1, :] for i in range(6)]
        low = [low_ref[0, i : i + 1, :] for i in range(4)]
        ls, rs = sign_s[0], sign_s[1]
        high = [x * rs for x in high[:4]] + high[4:]
        low = [x * ls for x in low[:2]] + low[2:]
        nu0, dnu0, _, _ = material(*own)
        nur, dnur, _, _ = material(*high)
        nul, dnul, zp, zd = material(low[0], own[0], low[1], own[2], low[2], low[3])
        k = 0.5 * (nul + nu0)
        dk = 0.5 * (dnul + dnu0)
        flux = k * zp
        dflux = k * zd + dk * zp
        pack = jnp.concatenate(
            [flux, dflux, dflux, dflux, high[0], high[2], nur, dnur], axis=0
        )
        for i in range(rows // LANES):
            piece = jnp.concatenate(
                [
                    jnp.broadcast_to(pack[0:1, i * LANES : (i + 1) * LANES], (LANES - 8, LANES)),
                    pack[:, i * LANES : (i + 1) * LANES],
                ],
                axis=0,
            )
            halo[i * LANES : (i + 1) * LANES, :] = jnp.transpose(piece)


    def load(ref, at):
        return [ref[0, pl.ds(at, 8), c * LANES : (c + 1) * LANES] for c in range(count)]

    def up(x, follow):
        return [
            pltpu.roll(jnp.where(at_top, y, z), 7, 0)
            for z, y in zip(x, follow)
        ]

    def down(x, before):
        return [
            pltpu.roll(jnp.where(at_bottom, y, z), 1, 0)
            for z, y in zip(x, before)
        ]

    def forward(x, end):
        turned = [pltpu.roll(z, LANES - 1, 1) for z in x]
        return [
            jnp.where(at_end, turned[c + 1] if c + 1 < count else end, turned[c])
            for c in range(count)
        ]

    def backward(x, start):
        turned = [pltpu.roll(z, 1, 1) for z in x]
        return [jnp.where(at_start, turned[c - 1] if c else start, turned[c]) for c in range(count)]

    def each(f, *xs):
        return [f(*x) for x in zip(*xs)]

    def material(a, v, a_down, v_down, reg, tab, h):
        rp = each(lambda x, y: y - x, a, a_down)
        rd = each(lambda x, y: y - x, v, v_down)
        zp = each(lambda x, y: y - x, a, forward(a, pltpu.roll(h, 3, 1)))
        zd = each(lambda x, y: y - x, v, forward(v, pltpu.roll(h, 2, 1)))

        def coefficients(rp, rd, zp, zd, reg, tab):
            base = jnp.take_along_axis(reg_tab, reg, axis=1, mode="promise_in_bounds")
            satur = jnp.take_along_axis(sat_tab, tab, axis=1, mode="promise_in_bounds")
            bs = base * satur
            return (
                0.5 * (base + bs * (rp * rp + zp * zp)),
                bs * (rp * rd + zp * zd),
            )

        both = each(coefficients, rp, rd, zp, zd, reg, tab)
        return [x[0] for x in both], [x[1] for x in both], rp, rd, zp, zd

    start_row = block * size

    def halo_at(at):
        return halo[pl.ds(pl.multiple_of(start_row + at, 8), 8), :]

    def emit(at, cur, h, nu_next, dnu_next, fr_before, dfr_before):
        nu, dnu, rp, rd, zp, zd = cur
        kr = each(lambda x, y: x + y, nu, up(nu, nu_next))
        dkr = each(lambda x, y: x + y, dnu, up(dnu, dnu_next))
        fr = each(lambda x, y: x * y, kr, rp)
        dfr = each(lambda k, d, dk, p: k * d + dk * p, kr, rd, dkr, rp)
        half = 0.5
        kf = each(lambda x, y: x + y, nu, forward(nu, half * pltpu.roll(h, 1, 1)))
        dkf = each(lambda x, y: x + y, dnu, forward(dnu, half * h))
        fz = each(lambda x, y: x * y, kf, zp)
        dfz = each(lambda k, d, dk, p: k * d + dk * p, kf, zd, dkf, zp)
        fr_up = down(fr, fr_before)
        dfr_up = down(dfr, dfr_before)
        fz_back = backward(fz, h)
        dfz_back = backward(dfz, pltpu.roll(h, LANES - 121, 1))
        for c in range(count):
            cut = slice(c * LANES, (c + 1) * LANES)
            where = (0, pl.ds(at, 8), cut)
            res_ref[where] = (fr_up[c] - fr[c]) + (fz_back[c] - fz[c]) - src_ref[where]
            jac_ref[where] = (dfr_up[c] - dfr[c]) + (dfz_back[c] - dfz[c])
        return fr, dfr

    def tile_material(at, a_after, v_after):
        a, v = load(a_ref, at), load(v_ref, at)
        h = halo_at(at)
        return material(
            a, v, up(a, a_after), up(v, v_after), load(r_ref, at), load(t_ref, at), h
        )

    cur = tile_material(0, load(a_ref, 8), load(v_ref, 8))

    @pl.when(block == 0)
    def _():
        a, v = load(a_ref, 0), load(v_ref, 0)
        for c in range(count):
            cut = slice(c * LANES, (c + 1) * LANES)
            inner = 2.0 * cur[0][c] * a[c]
            dinner = 2.0 * cur[0][c] * v[c] + 2.0 * cur[1][c] * a[c]
            carry_ref[0, :, cut] = pltpu.roll(inner, 7, 0)
            carry_ref[1, :, cut] = pltpu.roll(dinner, 7, 0)

    fr = [carry_ref[0, :, c * LANES : (c + 1) * LANES] for c in range(count)]
    dfr = [carry_ref[1, :, c * LANES : (c + 1) * LANES] for c in range(count)]

    def step(t, state):
        cur, fr, dfr = state
        at = pl.multiple_of(t * 8, 8)
        after = pl.multiple_of(t * 8 + 8, 8)
        beyond = pl.multiple_of(t * 8 + 16, 8)
        following = tile_material(after, load(a_ref, beyond), load(v_ref, beyond))
        fr, dfr = emit(at, cur, halo_at(at), following[0], following[1], fr, dfr)
        return following, fr, dfr

    cur, fr, dfr = lax.fori_loop(0, tiles - 2, step, (cur, fr, dfr), unroll=3)

    is_last = block == blocks - 1
    is_gap = start_row + size == RG
    end = size - 8

    def ending(ref, ext):
        own, beyond = load(ref, end), load(ext, 0)
        return each(
            lambda x, y: jnp.where(is_gap, pltpu.roll(x, 1, 0), jnp.where(is_last, 0.0, y)),
            own,
            beyond,
        )

    following = tile_material(end, ending(a_ref, ax), ending(v_ref, vx))
    fr, dfr = emit(end - 8, cur, halo_at(end - 8), following[0], following[1], fr, dfr)
    cur = following
    a, v = load(ax, 0), load(vx, 0)
    h = halo[pl.ds(pl.multiple_of(jnp.minimum(start_row + size, rows - 8), 8), 8), :]
    beyond = material(a, v, up(a, a), up(v, v), load(rx, 0), load(tx, 0), h)
    nu_next = each(lambda x, y: jnp.where(is_last, pltpu.roll(x, 1, 0), y), cur[0], beyond[0])
    dnu_next = each(lambda x, y: jnp.where(is_last, pltpu.roll(x, 1, 0), y), cur[1], beyond[1])
    fr, dfr = emit(end, cur, halo_at(end), nu_next, dnu_next, fr, dfr)
    for c in range(count):
        cut = slice(c * LANES, (c + 1) * LANES)
        carry_ref[0, :, cut] = fr[c]
        carry_ref[1, :, cut] = dfr[c]


BLOCK = 256


def stencil(potential, direction, source, regions, tables, reg, sat, signs, own, low, high):
    slices, rows, width = potential.shape
    blocks = rows // BLOCK
    whole = pl.BlockSpec((1, BLOCK, width), lambda s, i: (s, i, 0))
    after = pl.BlockSpec(
        (1, 8, width),
        lambda s, i: (s, jnp.minimum((i + 1) * (BLOCK // 8), rows // 8 - 1), 0),
    )
    edge = pl.BlockSpec((1, 8, rows), lambda s, i: (s, 0, 0))
    table = pl.BlockSpec((8, LANES), lambda s, i: (0, 0))
    smem = pl.BlockSpec(memory_space=pltpu.SMEM)
    regv = jnp.broadcast_to(jnp.pad(reg, (0, LANES - NREG)), (8, LANES))
    tabv = jnp.broadcast_to(jnp.pad(sat, (0, LANES - NTAB)), (8, LANES))
    return pl.pallas_call(
        stencil_kernel,
        grid=(slices, blocks),
        in_specs=[smem] * 3 + [table] * 2 + [edge] * 3 + [whole] * 5 + [after] * 4,
        out_specs=[whole, whole],
        out_shape=[jax.ShapeDtypeStruct(potential.shape, jnp.float32)] * 2,
        scratch_shapes=[
            pltpu.VMEM((rows, LANES), jnp.float32),
            pltpu.VMEM((2, 8, width), jnp.float32),
        ],
        compiler_params=pltpu.CompilerParams(vmem_limit_bytes=58 * 2**20),
        cost_estimate=pl.CostEstimate(
            flops=slices * rows * width * 60,
            bytes_accessed=slices * rows * width * 28,
            transcendentals=0,
        ),
    )(
        reg,
        sat,
        signs,
        regv,
        tabv,
        own,
        low,
        high,
        potential,
        direction,
        source,
        regions,
        tables,
        potential,
        direction,
        regions,
        tables,
    )


def gap_kernel(
    azims, mine, rows_ref, w1, tw, w2, w2i, w1i, gains, res_in, jac_in, res_ref, jac_ref, gap_ref,
    grid_z, grid_u, seen_ref,
):
    step = pl.program_id(0)
    devices, slices, _, count, _ = rows_ref.shape
    total = devices // azims * slices
    ka = tw.shape[1]
    own = mine[0]

    def dot(x, y):
        return jnp.dot(x, y, precision=highest, preferred_element_type=jnp.float32)

    @pl.when(step == 0)
    def _():
        owned = 2 * slices
        vectors = owned + 2 * total

        def gather(v, cut, s, q):
            for a in range(azims):
                grid_z[a * count : (a + 1) * count, v * LANES : (v + 1) * LANES] = rows_ref[
                    cut * azims + a, s, q
                ]

        for f in range(2):
            for s in range(slices):
                gather(f * slices + s, own, s, 2 * f)
            for s in range(total):
                gather(owned + f * total + s, s // slices, s % slices, 2 * f + 1)
        first = dot(w1[...], grid_z[...])
        tr, ti = tw[0], tw[1]
        for v in range(vectors):
            re = first[0:ka, v * LANES : (v + 1) * LANES]
            im = first[ka : 2 * ka, v * LANES : (v + 1) * LANES]
            grid_u[v * ka : (v + 1) * ka, 0:LANES] = re * tr - im * ti
            grid_u[v * ka : (v + 1) * ka, LANES : 2 * LANES] = re * ti + im * tr
        bins = dot(grid_u[...], w2[...])

        def part(v):
            return (
                bins[v * ka : (v + 1) * ka, 0:LANES],
                bins[v * ka : (v + 1) * ka, LANES : 2 * LANES],
            )

        k1 = lax.broadcasted_iota(jnp.int32, (ka, LANES), 0)
        k2 = lax.broadcasted_iota(jnp.int32, (ka, LANES), 1)
        freq = 4 * k1 + 4 * ka * k2 + 1
        period = 2 * ka * LANES

        def skew(cut, s):
            offset = jnp.broadcast_to(
                rows_ref[cut * azims, s, 4, 0:1, :].astype(jnp.int32), (ka, LANES)
            )
            angle = (freq * offset & (2 * period - 1)).astype(jnp.float32) * (math.pi / period)
            return jnp.cos(angle), jnp.sin(angle)

        axial = [[0.0, 0.0], [0.0, 0.0]]
        for s in range(total):
            c, d = skew(s // slices, s % slices)
            for f in range(2):
                re, im = part(owned + f * total + s)
                x, y = re * c - im * d, re * d + im * c
                seen_ref[s, f, 0] = x
                seen_ref[s, f, 1] = y
                axial[f][0] = axial[f][0] + x
                axial[f][1] = axial[f][1] + y
        self_gain, cross_gain = gains[0], gains[1]
        for s in range(slices):
            c, d = skew(own, s)
            for f in range(2):
                seen = [seen_ref[own * slices + s, f, i] for i in range(2)]
                rotor = part(f * slices + s)
                blended = [0.5 * (seen[i] + axial[f][i] * (1.0 / total)) for i in range(2)]
                flux = [self_gain * rotor[i] - cross_gain * blended[i] for i in range(2)]
                back = [self_gain * seen[i] - cross_gain * rotor[i] for i in range(2)]
                stator = (back[0] * c + back[1] * d, back[1] * c - back[0] * d)
                for r, value in enumerate((flux, stator)):
                    v = (f * slices + s) * 2 + r
                    grid_u[v * ka : (v + 1) * ka, 0:LANES] = value[0]
                    grid_u[v * ka : (v + 1) * ka, LANES : 2 * LANES] = value[1]
        outs = 4 * slices
        lines = dot(grid_u[0 : outs * ka, :], w2i[...])
        for v in range(outs):
            re = lines[v * ka : (v + 1) * ka, 0:LANES]
            im = lines[v * ka : (v + 1) * ka, LANES : 2 * LANES]
            grid_z[0:ka, v * LANES : (v + 1) * LANES] = re * tr + im * ti
            grid_z[ka : 2 * ka, v * LANES : (v + 1) * LANES] = im * tr - re * ti
        last = dot(w1i[...], grid_z[:, 0 : outs * LANES])
        for f in range(2):
            for s in range(slices):
                for r in range(2):
                    v = (f * slices + s) * 2 + r
                    for c in range(count):
                        gap_ref[f, s, r : r + 1, c * LANES : (c + 1) * LANES] = last[
                            c : c + 1, v * LANES : (v + 1) * LANES
                        ]

    width = res_in.shape[2]
    line = lax.broadcasted_iota(jnp.int32, (8, width), 0)
    for s in range(slices):
        for f, (old, new) in enumerate(((res_in, res_ref), (jac_in, jac_ref))):
            pair = gap_ref[f, s]
            add = jnp.where(step == 0, pair[0:1], pair[1:2])
            target = jnp.where(step == 0, 7, 0)
            new[s] = jnp.where(line == target, old[s] + add, old[s])


def gap(residual, jac_product, gathered, azims, mine, position):
    slices, rows, width = residual.shape
    devices = gathered.shape[0]
    count = width // LANES
    period = azims * width
    ka = period // (2 * LANES)
    w1, tw, w2, w2i, w1i, gains = transform_tables(period)
    lines = -(-count // 8) * 8
    w1i = np.pad(w1i, ((0, lines), (0, 0)))
    mine_w1i = lax.dynamic_slice_in_dim(jnp.asarray(w1i), position * count, lines, 0)
    total = devices // azims * slices
    vectors = 2 * slices + 2 * total
    touched = pl.BlockSpec((slices, 8, width), lambda g: (0, RG // 8 - 1 + g, 0))

    def full(x):
        zeros = (0,) * len(x.shape)
        return pl.BlockSpec(x.shape, lambda g: zeros)

    operands = [gathered] + [jnp.asarray(x) for x in (w1, tw, w2, w2i)]
    operands += [mine_w1i, jnp.asarray(gains)]
    shape = (2, slices, 2, width)
    return pl.pallas_call(
        functools.partial(gap_kernel, azims),
        grid=(2,),
        in_specs=[pl.BlockSpec(memory_space=pltpu.SMEM)]
        + [full(x) for x in operands]
        + [touched, touched],
        out_specs=[touched, touched, pl.BlockSpec(shape, lambda g: (0, 0, 0, 0))],
        out_shape=[
            jax.ShapeDtypeStruct(residual.shape, jnp.float32),
            jax.ShapeDtypeStruct(residual.shape, jnp.float32),
            jax.ShapeDtypeStruct(shape, jnp.float32),
        ],
        scratch_shapes=[
            pltpu.VMEM((2 * ka, vectors * LANES), jnp.float32),
            pltpu.VMEM((vectors * ka, 2 * LANES), jnp.float32),
            pltpu.VMEM((total, 2, 2, ka, LANES), jnp.float32),
        ],
        input_output_aliases={8: 0, 9: 1},
        compiler_params=pltpu.CompilerParams(vmem_limit_bytes=58 * 2**20),
        cost_estimate=pl.CostEstimate(
            flops=vectors * ka * 2 * LANES * 1000, bytes_accessed=2**21, transcendentals=0
        ),
    )(mine, *operands, residual, jac_product)


def body(
    potential, direction, source, region_ids, table_ids, region_reluct, table_sat, skew_offsets
):
    position = lax.axis_index("azim")
    azims = lax.axis_size("azim")
    left, right, rows = edges(potential, direction, region_ids, table_ids, skew_offsets)
    low, high, gathered = exchange(left, right, rows)
    gathered = gathered.reshape((-1,) + rows.shape)
    signs = jnp.stack(
        [jnp.where(position == 0, -1.0, 1.0), jnp.where(position == azims - 1, -1.0, 1.0)]
    ).astype(jnp.float32)
    residual, jac_product = stencil(
        potential,
        direction,
        source,
        region_ids,
        table_ids,
        region_reluct,
        table_sat,
        signs,
        left,
        low,
        high,
    )
    mine = lax.axis_index("cuts").astype(jnp.int32).reshape(1)
    return tuple(gap(residual, jac_product, gathered, azims, mine, position))


def solution(mesh):
    return jax.shard_map(
        body,
        mesh=mesh,
        in_specs=(
            P("cuts", None, "azim"),
            P("cuts", None, "azim"),
            P("cuts", None, "azim"),
            P("cuts", None, "azim"),
            P("cuts", None, "azim"),
            P(),
            P(),
            P("cuts"),
        ),
        out_specs=(P("cuts", None, "azim"), P("cuts", None, "azim"), P(None, "cuts", None, "azim")),
        check_vma=False,
    )
```

```python
import functools
import math

import jax
import jax.numpy as jnp
import numpy as np
from jax import lax
from jax.experimental import pallas as pl
from jax.experimental.pallas import tpu as pltpu
from jax.sharding import PartitionSpec as P

NREG = 8
NTAB = 16
RG = 512
GAP_SCALE = 4.0
LANES = 128
highest = lax.Precision.HIGHEST


def transform_tables(period):
    ka = period // (2 * LANES)
    a = np.arange(ka)
    b = np.arange(LANES)
    first = np.exp(-2j * np.pi * np.outer(a, a) / ka - 1j * np.pi * a[None, :] * LANES / period)
    w1 = np.block([[first.real, first.imag], [first.imag, -first.real]])
    twiddle = np.exp(
        -2j * np.pi * np.outer(a, b) / (ka * LANES) - 1j * np.pi * b[None, :] / period
    )
    second = np.exp(-2j * np.pi * np.outer(b, b) / LANES)
    w2 = np.block([[second.real, second.imag], [-second.imag, second.real]])
    back2 = np.conj(second)
    w2i = np.block([[back2.real, back2.imag], [-back2.imag, back2.real]])
    back1 = np.conj(first).T / (ka * LANES)
    w1i = np.block([[back1.real, -back1.imag], [-back1.imag, -back1.real]])
    freq = (4 * (a[:, None] + ka * b[None, :]) + 1) % (2 * period)
    odd = np.minimum(freq, 2 * period - freq)
    wave = GAP_SCALE * odd / period
    gains = np.stack([wave / np.tanh(wave), wave / np.sinh(wave)])
    twiddles = np.stack([twiddle.real, twiddle.imag])
    return [np.asarray(t, np.float32) for t in (w1, twiddles, w2, w2i, w1i, gains)]


def edge_kernel(
    off_ref, af, al, vf, vl, rf, rl, tf, tl, a0, a1, v0, v1, left_ref, right_ref, rows_ref
):
    s = pl.program_id(0)
    rows = af.shape[1]
    lane = lax.broadcasted_iota(jnp.int32, (LANES, LANES), 1)
    last = LANES - 1

    def pick(mix, ref, at, source, target):
        tile = ref[0, pl.ds(at, LANES), :].astype(jnp.float32)
        shift = (target - source) % LANES
        if shift:
            tile = pltpu.roll(tile, shift, 1)
        return jnp.where(lane == target, tile, mix)

    for block in range(rows // LANES):
        at = block * LANES
        mix = jnp.zeros((LANES, LANES), jnp.float32)
        tile = af[0, pl.ds(at, LANES), :]
        mix = jnp.where(lane < 2, tile, mix)
        tile = pltpu.roll(vf[0, pl.ds(at, LANES), :], 2, 1)
        mix = jnp.where((lane >= 2) & (lane < 4), tile, mix)
        mix = pick(mix, rf, at, 0, 4)
        mix = pick(mix, tf, at, 0, 5)
        mix = pick(mix, al, at, last, 8)
        mix = pick(mix, vl, at, last, 9)
        mix = pick(mix, rl, at, last, 10)
        mix = pick(mix, tl, at, last, 11)
        flat = jnp.transpose(mix)
        left_ref[0, :, pl.ds(at, LANES)] = flat[0:8]
        right_ref[0, :, pl.ds(at, LANES)] = flat[8:16]
    count = rows_ref.shape[2]
    for c in range(count):
        cut = pl.ds(c * LANES, LANES)
        rows_ref[3, 0, c : c + 1, :] = a0[0, 7:8, cut]
        rows_ref[0, 0, c : c + 1, :] = a1[0, 0:1, cut]
        rows_ref[4, 0, c : c + 1, :] = v0[0, 7:8, cut]
        rows_ref[1, 0, c : c + 1, :] = v1[0, 0:1, cut]
        rows_ref[2, 0, c : c + 1, :] = jnp.full((1, LANES), off_ref[s], jnp.int32).astype(
            jnp.float32
        )


def edges(potential, direction, regions, tables, offsets):
    slices, rows, width = potential.shape
    count = width // LANES
    first = pl.BlockSpec((1, rows, LANES), lambda s: (s, 0, 0))
    last = pl.BlockSpec((1, rows, LANES), lambda s: (s, 0, count - 1))
    rotor = pl.BlockSpec((1, 8, width), lambda s: (s, RG // 8 - 1, 0))
    stator = pl.BlockSpec((1, 8, width), lambda s: (s, RG // 8, 0))
    return pl.pallas_call(
        edge_kernel,
        grid=(slices,),
        in_specs=[pl.BlockSpec(memory_space=pltpu.SMEM)]
        + [first, last] * 4
        + [rotor, stator] * 2,
        out_specs=[
            pl.BlockSpec((1, 8, rows), lambda s: (s, 0, 0)),
            pl.BlockSpec((1, 8, rows), lambda s: (s, 0, 0)),
            pl.BlockSpec((5, 1, count, LANES), lambda s: (0, s, 0, 0)),
        ],
        out_shape=[
            jax.ShapeDtypeStruct((slices, 8, rows), jnp.float32),
            jax.ShapeDtypeStruct((slices, 8, rows), jnp.float32),
            jax.ShapeDtypeStruct((5, slices, count, LANES), jnp.float32),
        ],
        compiler_params=pltpu.CompilerParams(vmem_limit_bytes=58 * 2**20),
        cost_estimate=pl.CostEstimate(
            flops=slices * rows * 1000, bytes_accessed=slices * rows * 4096, transcendentals=0
        ),
    )(
        offsets,
        potential,
        potential,
        direction,
        direction,
        regions,
        regions,
        tables,
        tables,
        potential,
        potential,
        direction,
        direction,
    )


def exchange_kernel(
    azims, cuts, left, right, rows, low, high, gathered, edge_send, edge_recv, azim_send, azim_recv,
    cut_send, cut_recv,
):
    pos = lax.axis_index("azim")
    cut = lax.axis_index("cuts")
    mesh_id = pl.DeviceIdType.MESH

    def along(axis, here, number, k):
        return {axis: lax.rem(here + k, number)}

    peers = [along("azim", pos, azims, k) for k in range(1, azims)]
    others = [along("cuts", cut, cuts, k) for k in range(1, cuts)]
    barrier = pltpu.get_barrier_semaphore()
    for peer in peers + others:
        pl.semaphore_signal(barrier, inc=1, device_id=peer, device_id_type=mesh_id)
    pl.semaphore_wait(barrier, len(peers) + len(others))

    def send(src, dst, send_sem, recv_sem, peer):
        copy = pltpu.make_async_remote_copy(
            src_ref=src,
            dst_ref=dst,
            send_sem=send_sem,
            recv_sem=recv_sem,
            device_id=peer,
            device_id_type=mesh_id,
        )
        copy.start()
        return copy

    slot = gathered.at[cut, pos]
    inner = [
        send(rows, slot, azim_send.at[k], azim_recv.at[k], peer) for k, peer in enumerate(peers)
    ]
    borders = [
        send(right, low, edge_send.at[0], edge_recv.at[0], along("azim", pos, azims, 1)),
        send(left, high, edge_send.at[1], edge_recv.at[1], along("azim", pos, azims, azims - 1)),
    ]
    gathered[cut, pos] = rows[...]
    for copy in inner:
        copy.wait()
    shared = gathered.at[cut, :, 0:3]
    outer = [
        send(shared, shared, cut_send.at[k], cut_recv.at[k], peer)
        for k, peer in enumerate(others)
    ]
    for copy in borders + outer:
        copy.wait()


def exchange(left, right, rows):
    azims, cuts = lax.axis_size("azim"), lax.axis_size("cuts")
    vmem = pl.BlockSpec(memory_space=pltpu.VMEM)
    dma = pltpu.SemaphoreType.DMA
    return pl.pallas_call(
        functools.partial(exchange_kernel, azims, cuts),
        in_specs=[vmem] * 3,
        out_specs=[vmem] * 3,
        out_shape=[
            jax.ShapeDtypeStruct(left.shape, jnp.float32),
            jax.ShapeDtypeStruct(left.shape, jnp.float32),
            jax.ShapeDtypeStruct((cuts, azims) + rows.shape, jnp.float32),
        ],
        scratch_shapes=[dma((2,))] * 2 + [dma((azims - 1,))] * 2 + [dma((cuts - 1,))] * 2,
        compiler_params=pltpu.CompilerParams(
            collective_id=0, has_side_effects=True, vmem_limit_bytes=58 * 2**20
        ),
    )(left, right, rows)


def stencil_kernel(
    reg_s,
    tab_s,
    own_ref,
    low_ref,
    high_ref,
    a_ref,
    v_ref,
    src_ref,
    r_ref,
    t_ref,
    ax,
    vx,
    rx,
    tx,
    res_ref,
    jac_ref,
    halo,
    carry_ref,
):
    block = pl.program_id(1)
    blocks = pl.num_programs(1)
    size = a_ref.shape[1]
    count = a_ref.shape[2] // LANES
    rows = own_ref.shape[2]
    tiles = size // 8
    shape = (8, LANES)
    lane = lax.broadcasted_iota(jnp.int32, shape, 1)
    row = lax.broadcasted_iota(jnp.int32, shape, 0)
    at_end = lane == LANES - 1
    at_start = lane == 0
    at_bottom = row == 7
    at_top = row == 0
    reg_tab = jnp.zeros(shape, jnp.float32)
    for i in range(NREG):
        reg_tab = jnp.where(lane == i, reg_s[i], reg_tab)
    sat_tab = jnp.zeros(shape, jnp.float32)
    for i in range(NTAB):
        sat_tab = jnp.where(lane == i, tab_s[i], sat_tab)

    @pl.when(block == 0)
    def _():
        col = lax.broadcasted_iota(jnp.int32, (1, rows), 1)

        def pick(ids, table, number):
            total = jnp.zeros_like(ids)
            for i in range(number):
                total = jnp.where(ids == float(i), table[i], total)
            return total

        def material(a, a_next, v, v_next, reg, tab):
            def radial(x):
                follow = jnp.where(col == rows - 1, 0.0, pltpu.roll(x, rows - 1, 1))
                return jnp.where(col == RG - 1, 0.0, follow - x)

            base = pick(reg, reg_s, NREG)
            satur = pick(tab, tab_s, NTAB)
            rp, rd = radial(a), radial(v)
            zp, zd = a_next - a, v_next - v
            nu = base * (1.0 + satur * (rp * rp + zp * zp))
            dnu = 2.0 * base * satur * (rp * rd + zp * zd)
            return nu, dnu, zp, zd

        own = [own_ref[0, i : i + 1, :] for i in range(6)]
        high = [high_ref[0, i : i + 1, :] for i in range(6)]
        low = [low_ref[0, i : i + 1, :] for i in range(4)]
        position = lax.axis_index("azim")
        ls = jnp.where(position == 0, -1.0, 1.0)
        rs = jnp.where(position == lax.axis_size("azim") - 1, -1.0, 1.0)
        high = [x * rs for x in high[:4]] + high[4:]
        low = [x * ls for x in low[:2]] + low[2:]
        nu0, dnu0, _, _ = material(*own)
        nur, dnur, _, _ = material(*high)
        nul, dnul, zp, zd = material(low[0], own[0], low[1], own[2], low[2], low[3])
        k = 0.5 * (nul + nu0)
        dk = 0.5 * (dnul + dnu0)
        flux = k * zp
        dflux = k * zd + dk * zp
        pack = jnp.concatenate(
            [flux, dflux, dflux, dflux, high[0], high[2], nur, dnur], axis=0
        )
        for i in range(rows // LANES):
            piece = jnp.concatenate(
                [
                    jnp.broadcast_to(pack[0:1, i * LANES : (i + 1) * LANES], (LANES - 8, LANES)),
                    pack[:, i * LANES : (i + 1) * LANES],
                ],
                axis=0,
            )
            halo[i * LANES : (i + 1) * LANES, :] = jnp.transpose(piece)


    def load(ref, at):
        return [ref[0, pl.ds(at, 8), c * LANES : (c + 1) * LANES] for c in range(count)]

    def up(x, follow):
        return [
            pltpu.roll(jnp.where(at_top, y, z), 7, 0)
            for z, y in zip(x, follow)
        ]

    def down(x, before):
        return [
            pltpu.roll(jnp.where(at_bottom, y, z), 1, 0)
            for z, y in zip(x, before)
        ]

    def forward(x, end):
        turned = [pltpu.roll(z, LANES - 1, 1) for z in x]
        return [
            jnp.where(at_end, turned[c + 1] if c + 1 < count else end, turned[c])
            for c in range(count)
        ]

    def backward(x, start):
        turned = [pltpu.roll(z, 1, 1) for z in x]
        return [jnp.where(at_start, turned[c - 1] if c else start, turned[c]) for c in range(count)]

    def each(f, *xs):
        return [f(*x) for x in zip(*xs)]

    def material(a, v, a_down, v_down, reg, tab, h):
        rp = each(lambda x, y: y - x, a, a_down)
        rd = each(lambda x, y: y - x, v, v_down)
        zp = each(lambda x, y: y - x, a, forward(a, pltpu.roll(h, 3, 1)))
        zd = each(lambda x, y: y - x, v, forward(v, pltpu.roll(h, 2, 1)))

        def coefficients(rp, rd, zp, zd, reg, tab):
            base = jnp.take_along_axis(reg_tab, reg, axis=1, mode="promise_in_bounds")
            satur = jnp.take_along_axis(sat_tab, tab, axis=1, mode="promise_in_bounds")
            bs = base * satur
            return (
                0.5 * (base + bs * (rp * rp + zp * zp)),
                bs * (rp * rd + zp * zd),
            )

        both = each(coefficients, rp, rd, zp, zd, reg, tab)
        return [x[0] for x in both], [x[1] for x in both], rp, rd, zp, zd

    start_row = block * size

    def halo_at(at):
        return halo[pl.ds(pl.multiple_of(start_row + at, 8), 8), :]

    def emit(at, cur, h, nu_next, dnu_next, fr_before, dfr_before):
        nu, dnu, rp, rd, zp, zd = cur
        kr = each(lambda x, y: x + y, nu, up(nu, nu_next))
        dkr = each(lambda x, y: x + y, dnu, up(dnu, dnu_next))
        fr = each(lambda x, y: x * y, kr, rp)
        dfr = each(lambda k, d, dk, p: k * d + dk * p, kr, rd, dkr, rp)
        half = 0.5
        kf = each(lambda x, y: x + y, nu, forward(nu, half * pltpu.roll(h, 1, 1)))
        dkf = each(lambda x, y: x + y, dnu, forward(dnu, half * h))
        fz = each(lambda x, y: x * y, kf, zp)
        dfz = each(lambda k, d, dk, p: k * d + dk * p, kf, zd, dkf, zp)
        fr_up = down(fr, fr_before)
        dfr_up = down(dfr, dfr_before)
        fz_back = backward(fz, h)
        dfz_back = backward(dfz, pltpu.roll(h, LANES - 121, 1))
        for c in range(count):
            cut = slice(c * LANES, (c + 1) * LANES)
            where = (0, pl.ds(at, 8), cut)
            res_ref[where] = (fr_up[c] - fr[c]) + (fz_back[c] - fz[c]) - src_ref[where]
            jac_ref[where] = (dfr_up[c] - dfr[c]) + (dfz_back[c] - dfz[c])
        return fr, dfr

    def tile_material(at, a_after, v_after):
        a, v = load(a_ref, at), load(v_ref, at)
        h = halo_at(at)
        return material(
            a, v, up(a, a_after), up(v, v_after), load(r_ref, at), load(t_ref, at), h
        )

    cur = tile_material(0, load(a_ref, 8), load(v_ref, 8))

    @pl.when(block == 0)
    def _():
        a, v = load(a_ref, 0), load(v_ref, 0)
        for c in range(count):
            cut = slice(c * LANES, (c + 1) * LANES)
            inner = 2.0 * cur[0][c] * a[c]
            dinner = 2.0 * cur[0][c] * v[c] + 2.0 * cur[1][c] * a[c]
            carry_ref[0, :, cut] = pltpu.roll(inner, 7, 0)
            carry_ref[1, :, cut] = pltpu.roll(dinner, 7, 0)

    fr = [carry_ref[0, :, c * LANES : (c + 1) * LANES] for c in range(count)]
    dfr = [carry_ref[1, :, c * LANES : (c + 1) * LANES] for c in range(count)]

    def step(t, state):
        cur, fr, dfr = state
        at = pl.multiple_of(t * 8, 8)
        after = pl.multiple_of(t * 8 + 8, 8)
        beyond = pl.multiple_of(t * 8 + 16, 8)
        following = tile_material(after, load(a_ref, beyond), load(v_ref, beyond))
        fr, dfr = emit(at, cur, halo_at(at), following[0], following[1], fr, dfr)
        return following, fr, dfr

    cur, fr, dfr = lax.fori_loop(0, tiles - 2, step, (cur, fr, dfr), unroll=3)

    is_last = block == blocks - 1
    is_gap = start_row + size == RG
    end = size - 8

    def ending(ref, ext):
        own, beyond = load(ref, end), load(ext, 0)
        return each(
            lambda x, y: jnp.where(is_gap, pltpu.roll(x, 1, 0), jnp.where(is_last, 0.0, y)),
            own,
            beyond,
        )

    following = tile_material(end, ending(a_ref, ax), ending(v_ref, vx))
    fr, dfr = emit(end - 8, cur, halo_at(end - 8), following[0], following[1], fr, dfr)
    cur = following
    a, v = load(ax, 0), load(vx, 0)
    h = halo[pl.ds(pl.multiple_of(jnp.minimum(start_row + size, rows - 8), 8), 8), :]
    beyond = material(a, v, up(a, a), up(v, v), load(rx, 0), load(tx, 0), h)
    nu_next = each(lambda x, y: jnp.where(is_last, pltpu.roll(x, 1, 0), y), cur[0], beyond[0])
    dnu_next = each(lambda x, y: jnp.where(is_last, pltpu.roll(x, 1, 0), y), cur[1], beyond[1])
    fr, dfr = emit(end, cur, halo_at(end), nu_next, dnu_next, fr, dfr)
    for c in range(count):
        cut = slice(c * LANES, (c + 1) * LANES)
        carry_ref[0, :, cut] = fr[c]
        carry_ref[1, :, cut] = dfr[c]


BLOCK = 256


def stencil(potential, direction, source, regions, tables, reg, sat, own, low, high):
    slices, rows, width = potential.shape
    blocks = rows // BLOCK
    whole = pl.BlockSpec((1, BLOCK, width), lambda s, i: (s, i, 0))
    after = pl.BlockSpec(
        (1, 8, width),
        lambda s, i: (s, jnp.minimum((i + 1) * (BLOCK // 8), rows // 8 - 1), 0),
    )
    edge = pl.BlockSpec((1, 8, rows), lambda s, i: (s, 0, 0))
    smem = pl.BlockSpec(memory_space=pltpu.SMEM)
    return pl.pallas_call(
        stencil_kernel,
        grid=(slices, blocks),
        in_specs=[smem] * 2 + [edge] * 3 + [whole] * 5 + [after] * 4,
        out_specs=[whole, whole],
        out_shape=[jax.ShapeDtypeStruct(potential.shape, jnp.float32)] * 2,
        scratch_shapes=[
            pltpu.VMEM((rows, LANES), jnp.float32),
            pltpu.VMEM((2, 8, width), jnp.float32),
        ],
        compiler_params=pltpu.CompilerParams(vmem_limit_bytes=58 * 2**20),
        cost_estimate=pl.CostEstimate(
            flops=slices * rows * width * 60,
            bytes_accessed=slices * rows * width * 28,
            transcendentals=0,
        ),
    )(
        reg,
        sat,
        own,
        low,
        high,
        potential,
        direction,
        source,
        regions,
        tables,
        potential,
        direction,
        regions,
        tables,
    )


def gap_kernel(
    azims, rows_ref, w1, tw, w2, w2i, w1i, gains, res_in, jac_in, res_ref, jac_ref, gap_ref,
    grid_z, grid_u, seen_ref,
):
    step = pl.program_id(0)
    devices, _, slices, count, _ = rows_ref.shape
    total = devices // azims * slices
    ka = tw.shape[1]
    own = lax.axis_index("cuts")

    def dot(x, y):
        return jnp.dot(x, y, precision=highest, preferred_element_type=jnp.float32)

    @pl.when(step == 0)
    def _():
        owned = 2 * slices
        vectors = owned + 2 * total

        def gather(v, cut, s, q):
            for a in range(azims):
                grid_z[a * count : (a + 1) * count, v * LANES : (v + 1) * LANES] = rows_ref[
                    cut * azims + a, q, s
                ]

        for f in range(2):
            for s in range(slices):
                gather(f * slices + s, own, s, 3 + f)
            for s in range(total):
                gather(owned + f * total + s, s // slices, s % slices, f)
        first = dot(w1[...], grid_z[...])
        tr, ti = tw[0], tw[1]
        for v in range(vectors):
            re = first[0:ka, v * LANES : (v + 1) * LANES]
            im = first[ka : 2 * ka, v * LANES : (v + 1) * LANES]
            grid_u[v * ka : (v + 1) * ka, 0:LANES] = re * tr - im * ti
            grid_u[v * ka : (v + 1) * ka, LANES : 2 * LANES] = re * ti + im * tr
        bins = dot(grid_u[...], w2[...])

        def part(v):
            return (
                bins[v * ka : (v + 1) * ka, 0:LANES],
                bins[v * ka : (v + 1) * ka, LANES : 2 * LANES],
            )

        k1 = lax.broadcasted_iota(jnp.int32, (ka, LANES), 0)
        k2 = lax.broadcasted_iota(jnp.int32, (ka, LANES), 1)
        freq = 4 * k1 + 4 * ka * k2 + 1
        period = 2 * ka * LANES

        def skew(cut, s):
            offset = jnp.broadcast_to(
                rows_ref[cut * azims, 2, s, 0:1, :].astype(jnp.int32), (ka, LANES)
            )
            angle = (freq * offset & (2 * period - 1)).astype(jnp.float32) * (math.pi / period)
            return jnp.cos(angle), jnp.sin(angle)

        axial = [[0.0, 0.0], [0.0, 0.0]]
        for s in range(total):
            c, d = skew(s // slices, s % slices)
            for f in range(2):
                re, im = part(owned + f * total + s)
                x, y = re * c - im * d, re * d + im * c
                seen_ref[s, f, 0] = x
                seen_ref[s, f, 1] = y
                axial[f][0] = axial[f][0] + x
                axial[f][1] = axial[f][1] + y
        self_gain, cross_gain = gains[0], gains[1]
        for s in range(slices):
            c, d = skew(own, s)
            for f in range(2):
                seen = [seen_ref[own * slices + s, f, i] for i in range(2)]
                rotor = part(f * slices + s)
                blended = [0.5 * (seen[i] + axial[f][i] * (1.0 / total)) for i in range(2)]
                flux = [self_gain * rotor[i] - cross_gain * blended[i] for i in range(2)]
                back = [self_gain * seen[i] - cross_gain * rotor[i] for i in range(2)]
                stator = (back[0] * c + back[1] * d, back[1] * c - back[0] * d)
                for r, value in enumerate((flux, stator)):
                    v = (f * slices + s) * 2 + r
                    grid_u[v * ka : (v + 1) * ka, 0:LANES] = value[0]
                    grid_u[v * ka : (v + 1) * ka, LANES : 2 * LANES] = value[1]
        outs = 4 * slices
        lines = dot(grid_u[0 : outs * ka, :], w2i[...])
        for v in range(outs):
            re = lines[v * ka : (v + 1) * ka, 0:LANES]
            im = lines[v * ka : (v + 1) * ka, LANES : 2 * LANES]
            grid_z[0:ka, v * LANES : (v + 1) * LANES] = re * tr + im * ti
            grid_z[ka : 2 * ka, v * LANES : (v + 1) * LANES] = im * tr - re * ti
        last = dot(w1i[lax.axis_index("azim")], grid_z[:, 0 : outs * LANES])
        for f in range(2):
            for s in range(slices):
                for r in range(2):
                    v = (f * slices + s) * 2 + r
                    for c in range(count):
                        gap_ref[f, s, r : r + 1, c * LANES : (c + 1) * LANES] = last[
                            c : c + 1, v * LANES : (v + 1) * LANES
                        ]

    width = res_in.shape[2]
    line = lax.broadcasted_iota(jnp.int32, (8, width), 0)
    for s in range(slices):
        for f, (old, new) in enumerate(((res_in, res_ref), (jac_in, jac_ref))):
            pair = gap_ref[f, s]
            add = jnp.where(step == 0, pair[0:1], pair[1:2])
            target = jnp.where(step == 0, 7, 0)
            new[s] = jnp.where(line == target, old[s] + add, old[s])


def gap(residual, jac_product, gathered, azims):
    slices, rows, width = residual.shape
    devices = gathered.shape[0]
    count = width // LANES
    period = azims * width
    ka = period // (2 * LANES)
    w1, tw, w2, w2i, w1i, gains = transform_tables(period)
    lines = -(-count // 8) * 8
    w1i = w1i.reshape(azims, count, 2 * ka)
    w1i = np.pad(w1i, ((0, 0), (0, lines - count), (0, 0)))
    total = devices // azims * slices
    vectors = 2 * slices + 2 * total
    touched = pl.BlockSpec((slices, 8, width), lambda g: (0, RG // 8 - 1 + g, 0))

    def full(x):
        zeros = (0,) * len(x.shape)
        return pl.BlockSpec(x.shape, lambda g: zeros)

    operands = [gathered] + [jnp.asarray(x) for x in (w1, tw, w2, w2i)]
    operands += [jnp.asarray(w1i), jnp.asarray(gains)]
    shape = (2, slices, 2, width)
    return pl.pallas_call(
        functools.partial(gap_kernel, azims),
        grid=(2,),
        in_specs=[full(x) for x in operands] + [touched, touched],
        out_specs=[touched, touched, pl.BlockSpec(shape, lambda g: (0, 0, 0, 0))],
        out_shape=[
            jax.ShapeDtypeStruct(residual.shape, jnp.float32),
            jax.ShapeDtypeStruct(residual.shape, jnp.float32),
            jax.ShapeDtypeStruct(shape, jnp.float32),
        ],
        scratch_shapes=[
            pltpu.VMEM((2 * ka, vectors * LANES), jnp.float32),
            pltpu.VMEM((vectors * ka, 2 * LANES), jnp.float32),
            pltpu.VMEM((total, 2, 2, ka, LANES), jnp.float32),
        ],
        input_output_aliases={7: 0, 8: 1},
        compiler_params=pltpu.CompilerParams(vmem_limit_bytes=58 * 2**20),
        cost_estimate=pl.CostEstimate(
            flops=vectors * ka * 2 * LANES * 1000, bytes_accessed=2**21, transcendentals=0
        ),
    )(*operands, residual, jac_product)


def body(
    potential, direction, source, region_ids, table_ids, region_reluct, table_sat, skew_offsets
):
    azims = lax.axis_size("azim")
    left, right, rows = edges(potential, direction, region_ids, table_ids, skew_offsets)
    low, high, gathered = exchange(left, right, rows)
    gathered = gathered.reshape((-1,) + rows.shape)
    residual, jac_product = stencil(
        potential,
        direction,
        source,
        region_ids,
        table_ids,
        region_reluct,
        table_sat,
        left,
        low,
        high,
    )
    return tuple(gap(residual, jac_product, gathered, azims))


def solution(mesh):
    return jax.shard_map(
        body,
        mesh=mesh,
        in_specs=(
            P("cuts", None, "azim"),
            P("cuts", None, "azim"),
            P("cuts", None, "azim"),
            P("cuts", None, "azim"),
            P("cuts", None, "azim"),
            P(),
            P(),
            P("cuts"),
        ),
        out_specs=(P("cuts", None, "azim"), P("cuts", None, "azim"), P(None, "cuts", None, "azim")),
        check_vma=False,
    )
```
